1024 devices in a mesh: blk: 32 (over z_hi, x, core), group: 32 (over y, z_lo).
Axes of the slice: x: 4, y: 8, z: 16 (z_hi: 4, z_lo: 4; z = z_hi * 4 + z_lo), core: 2. Of those that a mesh axis runs over, the one named last changes fastest.
Arguments:
- images: bfloat16 [32, 32, 256, 1152], P('blk', 'group'), may hold values from -0.56640625 to 0.56640625
- texts: bfloat16 [32, 32, 256, 1152], P('blk', 'group'), may hold values from -0.56640625 to 0.56640625
Outputs:
- image_grad: float32 [32, 32, 256, 1152], P('blk', 'group')
- text_grad: float32 [32, 32, 256, 1152], P('blk', 'group')
The draws below stay inside these ranges and needn't reach their ends.
All inputs are finite; a program needn't handle non-finite values.
Results may differ from the reference program's by a relative error of at most 0.0018.
Values may be sent and summed in bfloat16 or wider, within the bound.
No kernel may reach another device: no remote copies, remote signals or barrier semaphores. Data moves between devices by JAX's collectives and lax.ppermute only.
A program may use at most 32 MiB of HBM per device.

```python
import jax
import jax.numpy as jnp
from jax import lax

D = 1152
ROWS = 256
HOPS = 2
N_BLK = 32
N_GROUP = 32


def block_scale(stream_key, shape, cuts, least, high):
    gain, own = 1.0, jax.random.fold_in(stream_key, 6)
    for position, parts in cuts:
        draws = jnp.exp(jax.random.uniform(jax.random.fold_in(own, position), (parts,), jnp.float32, least / len(cuts), high / len(cuts)))
        gain = gain * jnp.repeat(draws, shape[position] // parts).reshape([-1 if axis == position else 1 for axis in range(len(shape))])
    return gain


def centred(key, extent, spread, most, pieces=(), kind=jnp.bfloat16):
    level = block_scale(key, extent, pieces, -0.22, 0.18) if pieces else 1.0
    array = jax.random.normal(key, extent, jnp.float32) * spread * level
    return jnp.minimum(jnp.maximum(array, -most), most).astype(kind)


def setup_inputs(seed: int = 0) -> dict:
    seeds = jax.random.split(jax.random.key(seed), 3)
    return {
        "images": centred(seeds[0], (N_BLK, N_GROUP, ROWS, D), (0.5477 * D ** -0.25), 0.56640625, ((0, 32), (1, 32))),
        "texts": centred(seeds[1], (N_BLK, N_GROUP, ROWS, D), (0.5477 * D ** -0.25), 0.56640625, ((0, 32), (1, 32))),
    }


logit_scale = 10.0
logit_bias = -10.0


def tile_coef(image_tile, text_tile, positive):
    logits = logit_scale * jnp.einsum("gid,gjd->gij", image_tile.astype(jnp.float32), text_tile.astype(jnp.float32)) + logit_bias
    eye_matrix = jnp.eye(ROWS, dtype=jnp.float32)[None]
    coef = jax.nn.sigmoid(logits) - positive * eye_matrix
    coef = lax.optimization_barrier(coef.astype(jnp.bfloat16))
    return coef.astype(jnp.float32)


def reference(images, texts):
    def per_block(block):
        own_images = images[block]
        own_texts = texts[block]
        image_total = jnp.zeros(own_images.shape, jnp.float32)
        text_total = jnp.zeros(own_texts.shape, jnp.float32)
        for section_index in range(HOPS + 1):
            positive = 1.0 if section_index == 0 else 0.0
            earlier = (block - section_index) % N_BLK
            visiting = texts[earlier]
            coef = tile_coef(own_images, visiting, positive)
            image_total = image_total + logit_scale * jnp.einsum("gij,gjd->gid", coef, visiting.astype(jnp.float32))
            later = (block + section_index) % N_BLK
            far_images = images[later]
            coef_back = tile_coef(far_images, own_texts, positive)
            text_total = text_total + logit_scale * jnp.einsum("gij,gid->gjd", coef_back, far_images.astype(jnp.float32))
        return image_total, text_total

    image_grad, accum = lax.map(per_block, jnp.arange(N_BLK, dtype=jnp.int32))
    text_grad = jnp.roll(accum, (HOPS, 1), axis=(0, 1))
    return image_grad, text_grad
```

```python
import jax
import jax.numpy as jnp
from jax import lax
from jax.experimental import pallas as pl
from jax.experimental.pallas import tpu as pltpu
from jax.sharding import PartitionSpec as P

SCALE = 10.0
BIAS = -10.0
TOP = 13.0
EXTRA = 16
AXES = ("blk", "group")
NX, NY, NZ = 4, 8, 16


def place(x, y, z, c):
    x, y, z = x % NX, y % NY, z % NZ
    return ((z // 4) * 8 + x * 2 + c) * 32 + y * 4 + z % 4


def pairs(*moves):
    out = []
    for y in range(NY):
        for z in range(NZ):
            for (x0, c0), (x1, dz, c1) in moves:
                out.append((place(x0, y, z, c0), place(x1, y, z + dz, c1)))
    return out


PLANES = ((0, 2), (1, 0), (2, 1))
NEAR = [((x, c), (x + 1, 0, c)) for x in range(3) for c in range(2)]
STRAIGHT = [((3, c), (0, 4, c)) for c in range(2)]
MOVE_ALL = pairs(*NEAR, *STRAIGHT)
MOVE_NEAR = pairs(*NEAR)
MOVE_OUT = [pairs(*(((3, c), (p[c], 0, c)) for c in range(2))) for p in PLANES]
MOVE_ON = [pairs(*(((p[c], c), (0, 4, c)) for c in range(2))) for p in PLANES]
MOVE_SWAP = pairs(*(((x, c), (x, 0, 1 - c)) for x in range(4) for c in range(2)))


def move(value, table):
    return lax.ppermute(value, AXES, table)


def dot_nt(a, b):
    return lax.dot_general(a, b, (((1,), (1,)), ((), ())), preferred_element_type=jnp.float32)


def dot_tn(a, b):
    return lax.dot_general(a, b, (((0,), (0,)), ((), ())), preferred_element_type=jnp.float32)


def coefs(image, text, diagonal):
    out = jax.nn.sigmoid(SCALE * dot_nt(image, text) + BIAS)
    if diagonal:
        shape = out.shape
        eye = lax.broadcasted_iota(jnp.int32, shape, 0) == lax.broadcasted_iota(jnp.int32, shape, 1)
        out = out - eye.astype(jnp.float32)
    return out.astype(jnp.bfloat16)


def split_kernel(images, texts, i_a, i_b, t_a, t_b, rest, sems):
    half = i_a.shape[0]
    low, high = pl.ds(0, half), pl.ds(half, half)
    copies = [
        pltpu.make_async_copy(images.at[high], i_b, sems.at[0]),
        pltpu.make_async_copy(texts.at[low], t_a, sems.at[1]),
        pltpu.make_async_copy(texts.at[high], t_b, sems.at[2]),
        pltpu.make_async_copy(images.at[low], i_a, sems.at[3]),
        pltpu.make_async_copy(images.at[high], rest.at[pl.ds(0, half)], sems.at[4]),
        pltpu.make_async_copy(texts, rest.at[pl.ds(half, 2 * half)], sems.at[5]),
    ]
    for copy in copies:
        copy.start()
    for copy in copies:
        copy.wait()


def pick_kernel(where, head, rest, far0, far1, far2, i0, t0, i2, t2, swap):
    half = head.shape[0]
    i2[:half] = head[...]

    @pl.when(where[0] == 1)
    def _():
        i2[half:] = far0[...]
        t2[:half] = far1[...]
        t2[half:] = far2[...]

    @pl.when(where[0] == 0)
    def _():
        i2[half:] = rest[:half]
        t2[...] = rest[half:]

    @pl.when(where[1] == 1)
    def _():
        swap[: 2 * half] = i2[...]
        swap[2 * half :] = t2[...]

    @pl.when(where[1] == 0)
    def _():
        swap[: 2 * half] = i0[...]
        swap[2 * half :] = t0[...]


def two_kernel(i2, i0, t2, out):
    text = t2[...]
    out[...] = dot_tn(coefs(i2[...], text, True), i2[...]) + dot_tn(coefs(i0[...], text, False), i0[...])


def text_kernel(part, one, t2, code):
    rows = part.shape[0]
    acc = part[...] + dot_tn(coefs(one[:rows], t2[...], False), one[:rows])
    top = jnp.maximum(jnp.max(jnp.abs(acc), axis=(0, 1), keepdims=True), 1e-35)
    power = jnp.ceil(jnp.log2(top))
    z = acc * jnp.exp2(TOP - power)
    z2 = z * z
    z4 = z2 * z2
    code[:rows] = (z4 * z4 * z).astype(jnp.bfloat16)
    code[rows:] = jnp.broadcast_to(power, (code.shape[0] - rows, part.shape[1])).astype(jnp.bfloat16)


def read_kernel(code, out):
    step = out.shape[0]
    rows = code.shape[0] - EXTRA
    start = pl.multiple_of(pl.program_id(0) * step, step)
    y = code[pl.ds(start, step)].astype(jnp.float32)
    power = code[rows : rows + EXTRA].astype(jnp.float32)[:1, :1]
    z = jnp.exp2(jnp.log2(jnp.maximum(jnp.abs(y), 1e-38)) * (1.0 / 9.0)) * (SCALE * jnp.exp2(power - TOP))
    z = jnp.where(jnp.abs(y) < 2e-38, 0.0, z)
    out[...] = jnp.where(y < 0, -z, z)


def image_kernel(i0, t0, one, t2, out):
    rows = i0.shape[0]
    image = i0[...]
    acc = None
    for k, ref in enumerate((t0, one.at[rows:], t2)):
        text = ref[...]
        term = jnp.dot(coefs(image, text, k == 0), text, preferred_element_type=jnp.float32)
        acc = term if acc is None else acc + term
    out[...] = SCALE * acc


def body(images, texts):
    rows, width = images.shape[2:]
    half = rows // 2
    own_i = images.reshape(rows, width)
    own_t = texts.reshape(rows, width)
    blk = lax.axis_index("blk")
    core = blk % 2
    first = (blk // 2) % 4 == 0
    where = jnp.stack([first.astype(jnp.int32), core.astype(jnp.int32)])

    vm = pl.BlockSpec(memory_space=pltpu.VMEM)
    sm = pl.BlockSpec(memory_space=pltpu.SMEM)
    hbm = pl.BlockSpec(memory_space=pltpu.HBM)

    def call(kernel, outs, specs, terms, out_specs=vm, grid=(), scratch=()):
        return pl.pallas_call(
            kernel,
            out_shape=outs,
            in_specs=specs,
            out_specs=out_specs if not isinstance(outs, tuple) else (out_specs,) * len(outs),
            grid=grid,
            scratch_shapes=scratch,
            cost_estimate=pl.CostEstimate(
                flops=terms * 4 * rows * rows * width, bytes_accessed=2 << 20, transcendentals=0
            ),
            compiler_params=pltpu.CompilerParams(vmem_limit_bytes=32 << 20),
        )

    def bf(n):
        return jax.ShapeDtypeStruct((n, width), jnp.bfloat16)

    full = jax.ShapeDtypeStruct((rows, width), jnp.float32)

    i_a, i_b, t_a, t_b, near = call(
        split_kernel,
        (bf(half),) * 4 + (bf(3 * half),),
        [hbm] * 2,
        0,
        scratch=[pltpu.SemaphoreType.DMA((6,))],
    )(own_i, own_t)
    out = [move(p, t) for p, t in zip((i_b, t_a, t_b), MOVE_OUT)]
    head = move(i_a, MOVE_ALL)
    rest = move(near, MOVE_NEAR)
    far = [move(p, t) for p, t in zip(out, MOVE_ON)]
    i2, t2, swap = call(pick_kernel, (bf(rows), bf(rows), bf(2 * rows)), [sm] + [vm] * 7, 0)(
        where, head, rest, *far, own_i, own_t
    )
    one = move(swap, MOVE_SWAP)
    part = call(two_kernel, full, [vm] * 3, 2)(i2, own_i, t2)
    code = call(text_kernel, bf(rows + EXTRA), [vm] * 3, 1)(part, one, t2)
    count = lax.axis_size("group")
    got = lax.ppermute(code, "group", [(s, (s + 1) % count) for s in range(count)])
    image_grad = call(image_kernel, full, [vm] * 4, 3)(own_i, own_t, one, t2)
    cut = rows // 4
    text_grad = call(
        read_kernel, full, [vm], 0, out_specs=pl.BlockSpec((cut, width), lambda n: (n, 0)), grid=(rows // cut,)
    )(got)
    return image_grad.reshape(images.shape), text_grad.reshape(texts.shape)


def solution(mesh):
    spec = P("blk", "group", None, None)
    return jax.shard_map(body, mesh=mesh, in_specs=(spec, spec), out_specs=(spec, spec), check_vma=False)
```

```python
import jax
import jax.numpy as jnp
from jax import lax
from jax.experimental import pallas as pl
from jax.experimental.pallas import tpu as pltpu
from jax.sharding import PartitionSpec as P

SCALE = 10.0
BIAS = -10.0
TOP = 13.0
EXTRA = 16
AXES = ("blk", "group")
NX, NY, NZ = 4, 8, 16


def place(x, y, z, c):
    x, y, z = x % NX, y % NY, z % NZ
    return ((z // 4) * 8 + x * 2 + c) * 32 + y * 4 + z % 4


def pairs(*moves):
    out = []
    for y in range(NY):
        for z in range(NZ):
            for (x0, c0), (x1, dz, c1) in moves:
                out.append((place(x0, y, z, c0), place(x1, y, z + dz, c1)))
    return out


PLANES = ((0, 2), (1, 0), (2, 1))
NEAR = [((x, c), (x + 1, 0, c)) for x in range(3) for c in range(2)]
STRAIGHT = [((3, c), (0, 4, c)) for c in range(2)]
MOVE_ALL = pairs(*NEAR, *STRAIGHT)
MOVE_NEAR = pairs(*NEAR)
MOVE_OUT = [pairs(*(((3, c), (p[c], 0, c)) for c in range(2))) for p in PLANES]
MOVE_ON = [pairs(*(((p[c], c), (0, 4, c)) for c in range(2))) for p in PLANES]
MOVE_SWAP = pairs(*(((x, c), (x, 0, 1 - c)) for x in range(4) for c in range(2)))


def move(value, table):
    return lax.ppermute(value, AXES, table)


def dot_nt(a, b):
    return lax.dot_general(a, b, (((1,), (1,)), ((), ())), preferred_element_type=jnp.float32)


def dot_tn(a, b):
    return lax.dot_general(a, b, (((0,), (0,)), ((), ())), preferred_element_type=jnp.float32)


def coefs(image, text, diagonal):
    out = jax.nn.sigmoid(SCALE * dot_nt(image, text) + BIAS)
    if diagonal:
        shape = out.shape
        eye = lax.broadcasted_iota(jnp.int32, shape, 0) == lax.broadcasted_iota(jnp.int32, shape, 1)
        out = out - eye.astype(jnp.float32)
    return out.astype(jnp.bfloat16)


def near_kernel(images, texts, after0, after1, after2, rest, sems):
    half = after0.shape[0]
    high = pl.ds(half, half)
    copies = [
        pltpu.make_async_copy(images.at[high], rest.at[pl.ds(0, half)], sems.at[0]),
        pltpu.make_async_copy(texts, rest.at[pl.ds(half, 2 * half)], sems.at[1]),
    ]
    for copy in copies:
        copy.start()
    for copy in copies:
        copy.wait()


def pick_images(where, head, rest, far0, i0, i2, swap):
    half = head.shape[0]
    i2[:half] = head[...]

    @pl.when(where[0] == 1)
    def _():
        i2[half:] = far0[...]

    @pl.when(where[0] == 0)
    def _():
        i2[half:] = rest[:half]

    @pl.when(where[1] == 1)
    def _():
        swap[...] = i2[...]

    @pl.when(where[1] == 0)
    def _():
        swap[...] = i0[...]


def part_kernel(where, rest, far1, far2, i2, i0, t2, out):
    half = far1.shape[0]

    @pl.when(where[0] == 1)
    def _():
        t2[:half] = far1[...]
        t2[half:] = far2[...]

    @pl.when(where[0] == 0)
    def _():
        t2[...] = rest[half:]

    text = t2[...]
    out[...] = dot_tn(coefs(i2[...], text, True), i2[...]) + dot_tn(coefs(i0[...], text, False), i0[...])


def text_kernel(part, i1, t2, code):
    rows = part.shape[0]
    acc = part[...] + dot_tn(coefs(i1[...], t2[...], False), i1[...])
    top = jnp.maximum(jnp.max(jnp.abs(acc), axis=(0, 1), keepdims=True), 1e-35)
    power = jnp.ceil(jnp.log2(top))
    z = acc * jnp.exp2(TOP - power)
    z2 = z * z
    z4 = z2 * z2
    code[:rows] = (z4 * z4 * z).astype(jnp.bfloat16)
    code[rows:] = jnp.broadcast_to(power, (code.shape[0] - rows, acc.shape[1])).astype(jnp.bfloat16)


def pick_texts(where, code, t2, t0, swap):
    @pl.when(where[1] == 1)
    def _():
        swap[...] = t2[...]

    @pl.when(where[1] == 0)
    def _():
        swap[...] = t0[...]


def read_kernel(code, out):
    step = out.shape[0]
    rows = code.shape[0] - EXTRA
    start = pl.multiple_of(pl.program_id(0) * step, step)
    y = code[pl.ds(start, step)].astype(jnp.float32)
    power = code[rows : rows + EXTRA].astype(jnp.float32)[:1, :1]
    z = jnp.exp2(jnp.log2(jnp.maximum(jnp.abs(y), 1e-38)) * (1.0 / 9.0)) * (SCALE * jnp.exp2(power - TOP))
    z = jnp.where(jnp.abs(y) < 2e-38, 0.0, z)
    out[...] = jnp.where(y < 0, -z, z)


def image_kernel(i0, t0, t1, t2, out):
    image = i0[...]
    acc = None
    for k, ref in enumerate((t0, t1, t2)):
        text = ref[...]
        term = jnp.dot(coefs(image, text, k == 0), text, preferred_element_type=jnp.float32)
        acc = term if acc is None else acc + term
    out[...] = SCALE * acc


def body(images, texts):
    rows, width = images.shape[2:]
    half = rows // 2
    own_i = images.reshape(rows, width)
    own_t = texts.reshape(rows, width)
    blk = lax.axis_index("blk")
    core = blk % 2
    first = (blk // 2) % 4 == 0
    where = jnp.stack([first.astype(jnp.int32), core.astype(jnp.int32)])

    vm = pl.BlockSpec(memory_space=pltpu.VMEM)
    sm = pl.BlockSpec(memory_space=pltpu.SMEM)
    anywhere = pl.BlockSpec(memory_space=pl.ANY)

    def call(kernel, outs, specs, terms, out_specs=vm, grid=(), scratch=()):
        return pl.pallas_call(
            kernel,
            out_shape=outs,
            in_specs=specs,
            out_specs=out_specs if not isinstance(outs, tuple) else (out_specs,) * len(outs),
            grid=grid,
            scratch_shapes=scratch,
            cost_estimate=pl.CostEstimate(
                flops=terms * 4 * rows * rows * width, bytes_accessed=2 << 20, transcendentals=0
            ),
            compiler_params=pltpu.CompilerParams(vmem_limit_bytes=32 << 20),
        )

    def bf(n):
        return jax.ShapeDtypeStruct((n, width), jnp.bfloat16)

    full = jax.ShapeDtypeStruct((rows, width), jnp.float32)

    out = [move(p, t) for p, t in zip((own_i[half:], own_t[:half], own_t[half:]), MOVE_OUT)]
    head = move(own_i[:half], MOVE_ALL)
    near = call(
        near_kernel, bf(3 * half), [anywhere] * 5, 0, scratch=[pltpu.SemaphoreType.DMA((2,))]
    )(own_i, own_t, *out)
    rest = move(near, MOVE_NEAR)
    far = [move(p, t) for p, t in zip(out, MOVE_ON)]
    i2, swap_i = call(pick_images, (bf(rows),) * 2, [sm] + [vm] * 4, 0)(where, head, rest, far[0], own_i)
    i1 = move(swap_i, MOVE_SWAP)
    t2, part = call(part_kernel, (bf(rows), full), [sm] + [vm] * 5, 60)(where, rest, far[1], far[2], i2, own_i)
    code = call(text_kernel, bf(rows + EXTRA), [vm] * 3, 1)(part, i1, t2)
    count = lax.axis_size("group")
    got = lax.ppermute(code, "group", [(s, (s + 1) % count) for s in range(count)])
    t1 = move(call(pick_texts, bf(rows), [sm, anywhere] + [vm] * 2, 0)(where, code, t2, own_t), MOVE_SWAP)
    image_grad = call(image_kernel, full, [vm] * 4, 0)(own_i, own_t, t1, t2)
    cut = rows // 4
    text_grad = call(
        read_kernel, full, [vm], 0, out_specs=pl.BlockSpec((cut, width), lambda n: (n, 0)), grid=(rows // cut,)
    )(got)
    return image_grad.reshape(images.shape), text_grad.reshape(texts.shape)


def solution(mesh):
    spec = P("blk", "group", None, None)
    return jax.shard_map(body, mesh=mesh, in_specs=(spec, spec), out_specs=(spec, spec), check_vma=False)
```

```python
import jax
import jax.numpy as jnp
from jax import lax
from jax.experimental import pallas as pl
from jax.experimental.pallas import tpu as pltpu
from jax.sharding import PartitionSpec as P

SCALE = 10.0
BIAS = -10.0
TOP = 13.0
EXTRA = 16
AXES = ("blk", "group")
NX, NY, NZ = 4, 8, 16


def place(x, y, z, c):
    x, y, z = x % NX, y % NY, z % NZ
    return ((z // 4) * 8 + x * 2 + c) * 32 + y * 4 + z % 4


def pairs(*moves):
    out = []
    for y in range(NY):
        for z in range(NZ):
            for (x0, c0), (x1, dz, c1) in moves:
                out.append((place(x0, y, z, c0), place(x1, y, z + dz, c1)))
    return out


PLANES = ((0, 2), (1, 0), (2, 1))
CORES = range(2)
MOVE_ALL = pairs(*(((x, c), (x + 1, 0, c)) for x in range(3) for c in CORES), *(((3, c), (0, 4, c)) for c in CORES))
MOVE_OUT = [pairs(*(m for c in CORES for m in (((3, c), (p[c], 0, c)), ((p[c], c), (p[c] + 1, 0, c))))) for p in PLANES]
MOVE_ON = [
    pairs(*(((x, c), (0, 4, c) if x == p[c] else (x + 1, 0, c)) for x in range(3) for c in CORES)) for p in PLANES
]
MOVE_SWAP = pairs(*(((x, c), (x, 0, 1 - c)) for x in range(4) for c in CORES))


def move(value, table):
    return lax.ppermute(value, AXES, table)


def dot_nt(a, b):
    return lax.dot_general(a, b, (((1,), (1,)), ((), ())), preferred_element_type=jnp.float32)


def dot_tn(a, b):
    return lax.dot_general(a, b, (((0,), (0,)), ((), ())), preferred_element_type=jnp.float32)


def coefs(image, text, diagonal):
    out = jax.nn.sigmoid(SCALE * dot_nt(image, text) + BIAS)
    if diagonal:
        shape = out.shape
        eye = lax.broadcasted_iota(jnp.int32, shape, 0) == lax.broadcasted_iota(jnp.int32, shape, 1)
        out = out - eye.astype(jnp.float32)
    return out.astype(jnp.bfloat16)


def choose(flag, a, b, out):
    @pl.when(flag == 1)
    def _():
        out[...] = a[...]

    @pl.when(flag == 0)
    def _():
        out[...] = b[...]


def relay_kernel(relay, out, own, sent):
    choose(relay[0], out, own, sent)


def pick_images(where, head, out0, far0, i0, i2, swap):
    half = head.shape[0]
    i2[:half] = head[...]
    choose(where[1], out0, far0, i2.at[half:])
    choose(where[0], i2, i0, swap)


def part_kernel(where, out1, far1, out2, far2, i2, i0, t2, out):
    half = far1.shape[0]
    choose(where[2], out1, far1, t2.at[:half])
    choose(where[3], out2, far2, t2.at[half:])
    text = t2[...]
    out[...] = dot_tn(coefs(i2[...], text, True), i2[...]) + dot_tn(coefs(i0[...], text, False), i0[...])


def text_kernel(part, i1, t2, code):
    rows = part.shape[0]
    acc = part[...] + dot_tn(coefs(i1[...], t2[...], False), i1[...])
    top = jnp.maximum(jnp.max(jnp.abs(acc), axis=(0, 1), keepdims=True), 1e-35)
    power = jnp.ceil(jnp.log2(top))
    z = acc * jnp.exp2(TOP - power)
    z2 = z * z
    z4 = z2 * z2
    code[:rows] = (z4 * z4 * z).astype(jnp.bfloat16)
    code[rows:] = jnp.broadcast_to(power, (code.shape[0] - rows, acc.shape[1])).astype(jnp.bfloat16)


def pick_texts(where, code, t2, t0, swap):
    choose(where[0], t2, t0, swap)


def read_kernel(code, out):
    step = out.shape[0]
    rows = code.shape[0] - EXTRA
    start = pl.multiple_of(pl.program_id(0) * step, step)
    y = code[pl.ds(start, step)].astype(jnp.float32)
    power = code[rows : rows + EXTRA].astype(jnp.float32)[:1, :1]
    z = jnp.exp2(jnp.log2(jnp.maximum(jnp.abs(y), 1e-38)) * (1.0 / 9.0)) * (SCALE * jnp.exp2(power - TOP))
    z = jnp.where(jnp.abs(y) < 2e-38, 0.0, z)
    out[...] = jnp.where(y < 0, -z, z)


def image_kernel(i0, t0, t1, t2, out):
    image = i0[...]
    acc = None
    for k, ref in enumerate((t0, t1, t2)):
        text = ref[...]
        term = jnp.dot(coefs(image, text, k == 0), text, preferred_element_type=jnp.float32)
        acc = term if acc is None else acc + term
    out[...] = SCALE * acc


def body(images, texts):
    rows, width = images.shape[2:]
    half = rows // 2
    own_i = images.reshape(rows, width)
    own_t = texts.reshape(rows, width)
    blk = lax.axis_index("blk")
    core = blk % 2
    x = (blk // 2) % 4
    plane = [jnp.where(core == 0, *p) for p in PLANES]
    where = jnp.stack([core] + [(x == p + 1).astype(jnp.int32) for p in plane])

    vm = pl.BlockSpec(memory_space=pltpu.VMEM)
    sm = pl.BlockSpec(memory_space=pltpu.SMEM)
    anywhere = pl.BlockSpec(memory_space=pl.ANY)

    def call(kernel, outs, specs, terms, out_specs=vm, grid=(), scratch=()):
        return pl.pallas_call(
            kernel,
            out_shape=outs,
            in_specs=specs,
            out_specs=out_specs if not isinstance(outs, tuple) else (out_specs,) * len(outs),
            grid=grid,
            scratch_shapes=scratch,
            cost_estimate=pl.CostEstimate(
                flops=terms * 4 * rows * rows * width, bytes_accessed=2 << 20, transcendentals=0
            ),
            compiler_params=pltpu.CompilerParams(vmem_limit_bytes=32 << 20),
        )

    def bf(n):
        return jax.ShapeDtypeStruct((n, width), jnp.bfloat16)

    full = jax.ShapeDtypeStruct((rows, width), jnp.float32)

    pieces = (own_i[half:], own_t[:half], own_t[half:])
    out = [move(p, t) for p, t in zip(pieces, MOVE_OUT)]
    head = move(own_i[:half], MOVE_ALL)
    far = []
    for q, o, p, t in zip(plane, out, pieces, MOVE_ON):
        relay = (x == q).astype(jnp.int32).reshape(1)
        far.append(move(call(relay_kernel, bf(half), [sm] + [vm] * 2, 0)(relay, o, p), t))
    i2, swap_i = call(pick_images, (bf(rows),) * 2, [sm] + [vm] * 4, 0)(where, head, out[0], far[0], own_i)
    i1 = move(swap_i, MOVE_SWAP)
    t2, part = call(part_kernel, (bf(rows), full), [sm] + [vm] * 6, 60)(
        where, out[1], far[1], out[2], far[2], i2, own_i
    )
    code = call(text_kernel, bf(rows + EXTRA), [vm] * 3, 1)(part, i1, t2)
    count = lax.axis_size("group")
    got = lax.ppermute(code, "group", [(s, (s + 1) % count) for s in range(count)])
    t1 = move(call(pick_texts, bf(rows), [sm, anywhere] + [vm] * 2, 0)(where, code, t2, own_t), MOVE_SWAP)
    image_grad = call(image_kernel, full, [vm] * 4, 0)(own_i, own_t, t1, t2)
    cut = rows // 4
    text_grad = call(
        read_kernel, full, [vm], 0, out_specs=pl.BlockSpec((cut, width), lambda n: (n, 0)), grid=(rows // cut,)
    )(got)
    return image_grad.reshape(images.shape), text_grad.reshape(texts.shape)


def solution(mesh):
    spec = P("blk", "group", None, None)
    return jax.shard_map(body, mesh=mesh, in_specs=(spec, spec), out_specs=(spec, spec), check_vma=False)
```

```python
import jax
import jax.numpy as jnp
from jax import lax
from jax.experimental import pallas as pl
from jax.experimental.pallas import tpu as pltpu
from jax.sharding import PartitionSpec as P

SCALE = 10.0
BIAS = -10.0
TOP = 13.0
EXTRA = 16
AXES = ("blk", "group")
NX, NY, NZ = 4, 8, 16


def place(x, y, z, c):
    x, y, z = x % NX, y % NY, z % NZ
    return ((z // 4) * 8 + x * 2 + c) * 32 + y * 4 + z % 4


def pairs(*moves):
    out = []
    for y in range(NY):
        for z in range(NZ):
            for (x0, c0), (x1, dz, c1) in moves:
                out.append((place(x0, y, z, c0), place(x1, y, z + dz, c1)))
    return out


PLANES = ((0, 2), (1, 0), (2, 1))
CORES = range(2)
MOVE_STRAIGHT = pairs(*(((3, c), (0, 4, c)) for c in CORES))
MOVE_NEAR = pairs(*(((x, c), (x + 1, 0, c)) for x in range(3) for c in CORES))
MOVE_OUT = [pairs(*(m for c in CORES for m in (((3, c), (p[c], 0, c)), ((p[c], c), (p[c] + 1, 0, c))))) for p in PLANES]
MOVE_ON = [
    pairs(*(((x, c), (0, 4, c) if x == p[c] else (x + 1, 0, c)) for x in range(3) for c in CORES)) for p in PLANES
]
MOVE_SWAP = pairs(*(((x, c), (x, 0, 1 - c)) for x in range(4) for c in CORES))


def move(value, table):
    return lax.ppermute(value, AXES, table)


def dot_nt(a, b):
    return lax.dot_general(a, b, (((1,), (1,)), ((), ())), preferred_element_type=jnp.float32)


def dot_tn(a, b):
    return lax.dot_general(a, b, (((0,), (0,)), ((), ())), preferred_element_type=jnp.float32)


def coefs(image, text, diagonal):
    out = jax.nn.sigmoid(SCALE * dot_nt(image, text) + BIAS)
    if diagonal:
        shape = out.shape
        eye = lax.broadcasted_iota(jnp.int32, shape, 0) == lax.broadcasted_iota(jnp.int32, shape, 1)
        out = out - eye.astype(jnp.float32)
    return out.astype(jnp.bfloat16)


def choose(flag, a, b, out):
    @pl.when(flag == 1)
    def _():
        out[...] = a[...]

    @pl.when(flag == 0)
    def _():
        out[...] = b[...]


def relay_kernel(relay, out, own, sent):
    choose(relay[0], out, own, sent)


def after_kernel(own, after, sent):
    sent[...] = own[sent.shape[0] :]


def pick_images(where, out0, far0, out1, far1, i0, i2, swap):
    half = far0.shape[0]
    choose(where[1], out0, far0, i2.at[:half])
    choose(where[2], out1, far1, i2.at[half:])
    choose(where[0], i2, i0, swap)


def pick_texts(where, out2, far2, straight, picked):
    half = far2.shape[0]
    choose(where[3], out2, far2, picked.at[:half])
    picked[half:] = straight[...]


def part_kernel(where, picked, near, i2, i0, t2, out):
    half = near.shape[0]
    t2[:half] = picked[:half]
    choose(where[4], picked.at[half:], near, t2.at[half:])
    text = t2[...]
    out[...] = dot_tn(coefs(i2[...], text, True), i2[...]) + dot_tn(coefs(i0[...], text, False), i0[...])


def text_kernel(part, i1, t2, code):
    rows = part.shape[0]
    acc = part[...] + dot_tn(coefs(i1[...], t2[...], False), i1[...])
    top = jnp.maximum(jnp.max(jnp.abs(acc), axis=(0, 1), keepdims=True), 1e-35)
    power = jnp.ceil(jnp.log2(top))
    z = acc * jnp.exp2(TOP - power)
    z2 = z * z
    z4 = z2 * z2
    code[:rows] = (z4 * z4 * z).astype(jnp.bfloat16)
    code[rows:] = jnp.broadcast_to(power, (code.shape[0] - rows, acc.shape[1])).astype(jnp.bfloat16)


def swap_texts(where, code, t2, t0, swap):
    choose(where[0], t2, t0, swap)


def read_kernel(code, out):
    step = out.shape[0]
    rows = code.shape[0] - EXTRA
    start = pl.multiple_of(pl.program_id(0) * step, step)
    y = code[pl.ds(start, step)].astype(jnp.float32)
    power = code[rows : rows + EXTRA].astype(jnp.float32)[:1, :1]
    z = jnp.exp2(jnp.log2(jnp.maximum(jnp.abs(y), 1e-38)) * (1.0 / 9.0)) * (SCALE * jnp.exp2(power - TOP))
    z = jnp.where(jnp.abs(y) < 2e-38, 0.0, z)
    out[...] = jnp.where(y < 0, -z, z)


def image_kernel(i0, t0, t1, t2, out):
    image = i0[...]
    acc = None
    for k, ref in enumerate((t0, t1, t2)):
        text = ref[...]
        term = jnp.dot(coefs(image, text, k == 0), text, preferred_element_type=jnp.float32)
        acc = term if acc is None else acc + term
    out[...] = SCALE * acc


def body(images, texts):
    rows, width = images.shape[2:]
    half = rows // 2
    own_i = images.reshape(rows, width)
    own_t = texts.reshape(rows, width)
    blk = lax.axis_index("blk")
    core = blk % 2
    x = (blk // 2) % 4
    plane = [jnp.where(core == 0, *p) for p in PLANES]
    where = jnp.stack([core] + [(x == p + 1).astype(jnp.int32) for p in plane] + [(x == 0).astype(jnp.int32)])

    vm = pl.BlockSpec(memory_space=pltpu.VMEM)
    sm = pl.BlockSpec(memory_space=pltpu.SMEM)
    anywhere = pl.BlockSpec(memory_space=pl.ANY)

    def call(kernel, outs, specs, terms, out_specs=vm, grid=(), scratch=()):
        return pl.pallas_call(
            kernel,
            out_shape=outs,
            in_specs=specs,
            out_specs=out_specs if not isinstance(outs, tuple) else (out_specs,) * len(outs),
            grid=grid,
            scratch_shapes=scratch,
            cost_estimate=pl.CostEstimate(
                flops=terms * 4 * rows * rows * width, bytes_accessed=2 << 20, transcendentals=0
            ),
            compiler_params=pltpu.CompilerParams(vmem_limit_bytes=32 << 20),
        )

    def bf(n):
        return jax.ShapeDtypeStruct((n, width), jnp.bfloat16)

    full = jax.ShapeDtypeStruct((rows, width), jnp.float32)

    pieces = (own_i[:half], own_i[half:], own_t[:half])
    out = [move(p, t) for p, t in zip(pieces, MOVE_OUT)]
    straight = move(own_t[half:], MOVE_STRAIGHT)
    far = []
    for q, o, p, t in zip(plane, out, pieces, MOVE_ON):
        relay = (x == q).astype(jnp.int32).reshape(1)
        far.append(move(call(relay_kernel, bf(half), [sm] + [vm] * 2, 0)(relay, o, p), t))
    near = move(call(after_kernel, bf(half), [vm, anywhere], 0)(own_t, out[2]), MOVE_NEAR)
    i2, swap_i = call(pick_images, (bf(rows),) * 2, [sm] + [vm] * 5, 0)(where, out[0], far[0], out[1], far[1], own_i)
    i1 = move(swap_i, MOVE_SWAP)
    picked = call(pick_texts, bf(rows), [sm] + [vm] * 3, 20)(where, out[2], far[2], straight)
    t2, part = call(part_kernel, (bf(rows), full), [sm] + [vm] * 4, 60)(where, picked, near, i2, own_i)
    code = call(text_kernel, bf(rows + EXTRA), [vm] * 3, 1)(part, i1, t2)
    count = lax.axis_size("group")
    got = lax.ppermute(code, "group", [(s, (s + 1) % count) for s in range(count)])
    t1 = move(call(swap_texts, bf(rows), [sm, anywhere] + [vm] * 2, 0)(where, code, t2, own_t), MOVE_SWAP)
    image_grad = call(image_kernel, full, [vm] * 4, 0)(own_i, own_t, t1, t2)
    cut = rows // 4
    text_grad = call(
        read_kernel, full, [vm], 0, out_specs=pl.BlockSpec((cut, width), lambda n: (n, 0)), grid=(rows // cut,)
    )(got)
    return image_grad.reshape(images.shape), text_grad.reshape(texts.shape)


def solution(mesh):
    spec = P("blk", "group", None, None)
    return jax.shard_map(body, mesh=mesh, in_specs=(spec, spec), out_specs=(spec, spec), check_vma=False)
```

```python
import jax
import jax.numpy as jnp
from jax import lax
from jax.experimental import pallas as pl
from jax.experimental.pallas import tpu as pltpu
from jax.sharding import PartitionSpec as P

SCALE = 10.0
BIAS = -10.0
TOP = 13.0
EXTRA = 16
AXES = ("blk", "group")
NX, NY, NZ = 4, 8, 16


def place(x, y, z, c):
    x, y, z = x % NX, y % NY, z % NZ
    return ((z // 4) * 8 + x * 2 + c) * 32 + y * 4 + z % 4


def pairs(*moves):
    out = []
    for y in range(NY):
        for z in range(NZ):
            for (x0, c0), (x1, dz, c1) in moves:
                out.append((place(x0, y, z, c0), place(x1, y, z + dz, c1)))
    return out


PLANES = ((0, 2), (1, 0), (2, 1))
CORES = range(2)
MOVE_STRAIGHT = pairs(*(((3, c), (0, 4, c)) for c in CORES))
MOVE_NEAR = pairs(*(((x, c), (x + 1, 0, c)) for x in range(3) for c in CORES))
MOVE_OUT = [pairs(*(((3, c), (p[c], 0, c)) for c in CORES)) for p in PLANES]
MOVE_ON = [pairs(*(((p[c], c), (0, 4, c)) for c in CORES)) for p in PLANES]
MOVE_SWAP = pairs(*(((x, c), (x, 0, 1 - c)) for x in range(4) for c in CORES))


def move(value, table):
    return lax.ppermute(value, AXES, table)


def dot_nt(a, b):
    return lax.dot_general(a, b, (((1,), (1,)), ((), ())), preferred_element_type=jnp.float32)


def dot_tn(a, b):
    return lax.dot_general(a, b, (((0,), (0,)), ((), ())), preferred_element_type=jnp.float32)


def coefs(image, text, diagonal):
    out = jax.nn.sigmoid(SCALE * dot_nt(image, text) + BIAS)
    if diagonal:
        shape = out.shape
        eye = lax.broadcasted_iota(jnp.int32, shape, 0) == lax.broadcasted_iota(jnp.int32, shape, 1)
        out = out - eye.astype(jnp.float32)
    return out.astype(jnp.bfloat16)


def choose(flag, a, b, out):
    @pl.when(flag == 1)
    def _():
        out[...] = a[...]

    @pl.when(flag == 0)
    def _():
        out[...] = b[...]


def near_kernel(images, texts, both, sems):
    rows = images.shape[0]
    copies = [
        pltpu.make_async_copy(images, both.at[pl.ds(0, rows)], sems.at[0]),
        pltpu.make_async_copy(texts, both.at[pl.ds(rows, rows)], sems.at[1]),
    ]
    for copy in copies:
        copy.start()
    for copy in copies:
        copy.wait()


def far_kernel(far0, far1, far2, straight, images):
    half = far0.shape[0]
    images[:half] = far0[...]
    images[half:] = far1[...]


def pick_images(where, far, near, i0, i2, swap):
    rows = i0.shape[0]
    choose(where[1], far, near.at[:rows], i2)
    choose(where[0], i2, i0, swap)


def part_kernel(where, far2, straight, near, i2, i0, t2, out):
    half = far2.shape[0]
    choose(where[1], far2, near.at[2 * half : 3 * half], t2.at[:half])
    choose(where[1], straight, near.at[3 * half :], t2.at[half:])
    text = t2[...]
    out[...] = dot_tn(coefs(i2[...], text, True), i2[...]) + dot_tn(coefs(i0[...], text, False), i0[...])


def text_kernel(part, i1, t2, code):
    rows = part.shape[0]
    acc = part[...] + dot_tn(coefs(i1[...], t2[...], False), i1[...])
    top = jnp.maximum(jnp.max(jnp.abs(acc), axis=(0, 1), keepdims=True), 1e-35)
    power = jnp.ceil(jnp.log2(top))
    z = acc * jnp.exp2(TOP - power)
    z2 = z * z
    z4 = z2 * z2
    code[:rows] = (z4 * z4 * z).astype(jnp.bfloat16)
    code[rows:] = jnp.broadcast_to(power, (code.shape[0] - rows, acc.shape[1])).astype(jnp.bfloat16)


def pick_texts(where, code, t2, t0, swap):
    choose(where[0], t2, t0, swap)


def read_kernel(code, out):
    step = out.shape[0]
    rows = code.shape[0] - EXTRA
    start = pl.multiple_of(pl.program_id(0) * step, step)
    y = code[pl.ds(start, step)].astype(jnp.float32)
    power = code[rows : rows + EXTRA].astype(jnp.float32)[:1, :1]
    z = jnp.exp2(jnp.log2(jnp.maximum(jnp.abs(y), 1e-38)) * (1.0 / 9.0)) * (SCALE * jnp.exp2(power - TOP))
    z = jnp.where(jnp.abs(y) < 2e-38, 0.0, z)
    out[...] = jnp.where(y < 0, -z, z)


def image_kernel(i0, t0, t1, t2, out):
    image = i0[...]
    acc = None
    for k, ref in enumerate((t0, t1, t2)):
        text = ref[...]
        term = jnp.dot(coefs(image, text, k == 0), text, preferred_element_type=jnp.float32)
        acc = term if acc is None else acc + term
    out[...] = SCALE * acc


def body(images, texts):
    rows, width = images.shape[2:]
    half = rows // 2
    own_i = images.reshape(rows, width)
    own_t = texts.reshape(rows, width)
    blk = lax.axis_index("blk")
    core = blk % 2
    x = (blk // 2) % 4
    where = jnp.stack([core, (x == 0).astype(jnp.int32)])

    vm = pl.BlockSpec(memory_space=pltpu.VMEM)
    sm = pl.BlockSpec(memory_space=pltpu.SMEM)
    anywhere = pl.BlockSpec(memory_space=pl.ANY)

    def call(kernel, outs, specs, terms, out_specs=vm, grid=(), scratch=()):
        return pl.pallas_call(
            kernel,
            out_shape=outs,
            in_specs=specs,
            out_specs=out_specs if not isinstance(outs, tuple) else (out_specs,) * len(outs),
            grid=grid,
            scratch_shapes=scratch,
            cost_estimate=pl.CostEstimate(
                flops=terms * 4 * rows * rows * width, bytes_accessed=2 << 20, transcendentals=0
            ),
            compiler_params=pltpu.CompilerParams(vmem_limit_bytes=32 << 20),
        )

    def bf(n):
        return jax.ShapeDtypeStruct((n, width), jnp.bfloat16)

    full = jax.ShapeDtypeStruct((rows, width), jnp.float32)

    pieces = (own_i[:half], own_i[half:], own_t[:half])
    out = [move(p, t) for p, t in zip(pieces, MOVE_OUT)]
    straight = move(own_t[half:], MOVE_STRAIGHT)
    far = [move(o, t) for o, t in zip(out, MOVE_ON)]
    both = call(near_kernel, bf(2 * rows), [anywhere] * 2, 0, scratch=[pltpu.SemaphoreType.DMA((2,))])(own_i, own_t)
    near = move(both, MOVE_NEAR)
    beyond = call(far_kernel, bf(rows), [vm, vm, anywhere, anywhere], 36)(*far, straight)
    i2, swap_i = call(pick_images, (bf(rows),) * 2, [sm] + [vm] * 3, 0)(where, beyond, near, own_i)
    i1 = move(swap_i, MOVE_SWAP)
    t2, part = call(part_kernel, (bf(rows), full), [sm] + [vm] * 5, 2)(where, far[2], straight, near, i2, own_i)
    code = call(text_kernel, bf(rows + EXTRA), [vm] * 3, 1)(part, i1, t2)
    count = lax.axis_size("group")
    got = lax.ppermute(code, "group", [(s, (s + 1) % count) for s in range(count)])
    t1 = move(call(pick_texts, bf(rows), [sm, anywhere] + [vm] * 2, 0)(where, code, t2, own_t), MOVE_SWAP)
    image_grad = call(image_kernel, full, [vm] * 4, 0)(own_i, own_t, t1, t2)
    cut = rows // 4
    text_grad = call(
        read_kernel, full, [vm], 0, out_specs=pl.BlockSpec((cut, width), lambda n: (n, 0)), grid=(rows // cut,)
    )(got)
    return image_grad.reshape(images.shape), text_grad.reshape(texts.shape)


def solution(mesh):
    spec = P("blk", "group", None, None)
    return jax.shard_map(body, mesh=mesh, in_specs=(spec, spec), out_specs=(spec, spec), check_vma=False)
```

```python
import jax
import jax.numpy as jnp
from jax import lax
from jax.experimental import pallas as pl
from jax.experimental.pallas import tpu as pltpu
from jax.sharding import PartitionSpec as P

SCALE = 10.0
BIAS = -10.0
TOP = 13.0
EXTRA = 16
AXES = ("blk", "group")
NX, NY, NZ = 4, 8, 16


def place(x, y, z, c):
    x, y, z = x % NX, y % NY, z % NZ
    return ((z // 4) * 8 + x * 2 + c) * 32 + y * 4 + z % 4


def pairs(*moves):
    out = []
    for y in range(NY):
        for z in range(NZ):
            for (x0, c0), (x1, dz, c1) in moves:
                out.append((place(x0, y, z, c0), place(x1, y, z + dz, c1)))
    return out


PLANES = ((0, 2), (1, 0), (2, 1))
CORES = range(2)
MOVE_STRAIGHT = pairs(*(((3, c), (0, 4, c)) for c in CORES))
MOVE_NEAR = pairs(*(((x, c), (x + 1, 0, c)) for x in range(3) for c in CORES))
MOVE_OUT = [pairs(*(m for c in CORES for m in (((3, c), (p[c], 0, c)), ((p[c], c), (p[c] + 1, 0, c))))) for p in PLANES]
MOVE_ON = [
    pairs(*(((x, c), (0, 4, c) if x == p[c] else (x + 1, 0, c)) for x in range(3) for c in CORES)) for p in PLANES
]
MOVE_SWAP = pairs(*(((x, c), (x, 0, 1 - c)) for x in range(4) for c in CORES))


def move(value, table):
    return lax.ppermute(value, AXES, table)


def dot_nt(a, b):
    return lax.dot_general(a, b, (((1,), (1,)), ((), ())), preferred_element_type=jnp.float32)


def dot_tn(a, b):
    return lax.dot_general(a, b, (((0,), (0,)), ((), ())), preferred_element_type=jnp.float32)


def coefs(image, text, diagonal):
    out = jax.nn.sigmoid(SCALE * dot_nt(image, text) + BIAS)
    if diagonal:
        shape = out.shape
        eye = lax.broadcasted_iota(jnp.int32, shape, 0) == lax.broadcasted_iota(jnp.int32, shape, 1)
        out = out - eye.astype(jnp.float32)
    return out.astype(jnp.bfloat16)


def choose(flag, a, b, out):
    @pl.when(flag == 1)
    def _():
        out[...] = a[...]

    @pl.when(flag == 0)
    def _():
        out[...] = b[...]


def relay_kernel(relay, out, own, sent):
    choose(relay[0], out, own, sent)


def after_kernel(own, after, sent):
    sent[...] = own[own.shape[0] - sent.shape[0] :]


def swap_images(where, out0, far0, out1, far1, i0, swap):
    half = far0.shape[0]

    @pl.when(where[0] == 1)
    def _():
        choose(where[1], out0, far0, swap.at[:half])
        choose(where[2], out1, far1, swap.at[half:])

    @pl.when(where[0] == 0)
    def _():
        swap[...] = i0[...]


def all_kernel(far2, straight, swap, done):
    done[...] = jnp.zeros_like(done)


def part_kernel(where, done, out0, far0, out1, far1, out2, far2, straight, near, i0, t2, out, i2):
    half, cut = far0.shape[0], far2.shape[0]
    choose(where[1], out0, far0, i2.at[:half])
    choose(where[2], out1, far1, i2.at[half:])
    choose(where[3], out2, far2, t2.at[:cut])
    choose(where[4], straight, near, t2.at[cut:])
    text = t2[...]
    out[...] = dot_tn(coefs(i2[...], text, True), i2[...]) + dot_tn(coefs(i0[...], text, False), i0[...])


def text_kernel(part, i1, t2, code):
    rows = part.shape[0]
    acc = part[...] + dot_tn(coefs(i1[...], t2[...], False), i1[...])
    top = jnp.maximum(jnp.max(jnp.abs(acc), axis=(0, 1), keepdims=True), 1e-35)
    power = jnp.ceil(jnp.log2(top))
    z = acc * jnp.exp2(TOP - power)
    z2 = z * z
    z4 = z2 * z2
    code[:rows] = (z4 * z4 * z).astype(jnp.bfloat16)
    code[rows:] = jnp.broadcast_to(power, (code.shape[0] - rows, acc.shape[1])).astype(jnp.bfloat16)


def swap_texts(where, code, t2, t0, swap):
    choose(where[0], t2, t0, swap)


def read_kernel(code, out):
    step = out.shape[0]
    rows = code.shape[0] - EXTRA
    start = pl.multiple_of(pl.program_id(0) * step, step)
    y = code[pl.ds(start, step)].astype(jnp.float32)
    power = code[rows : rows + EXTRA].astype(jnp.float32)[:1, :1]
    z = jnp.exp2(jnp.log2(jnp.maximum(jnp.abs(y), 1e-38)) * (1.0 / 9.0)) * (SCALE * jnp.exp2(power - TOP))
    z = jnp.where(jnp.abs(y) < 2e-38, 0.0, z)
    out[...] = jnp.where(y < 0, -z, z)


def image_kernel(i0, t0, t1, t2, out):
    image = i0[...]
    acc = None
    for k, ref in enumerate((t0, t1, t2)):
        text = ref[...]
        term = jnp.dot(coefs(image, text, k == 0), text, preferred_element_type=jnp.float32)
        acc = term if acc is None else acc + term
    out[...] = SCALE * acc


def body(images, texts):
    rows, width = images.shape[2:]
    half = rows // 2
    own_i = images.reshape(rows, width)
    own_t = texts.reshape(rows, width)
    blk = lax.axis_index("blk")
    core = blk % 2
    x = (blk // 2) % 4
    plane = [jnp.where(core == 0, *p) for p in PLANES]
    where = jnp.stack([core] + [(x == p + 1).astype(jnp.int32) for p in plane] + [(x == 0).astype(jnp.int32)])

    vm = pl.BlockSpec(memory_space=pltpu.VMEM)
    sm = pl.BlockSpec(memory_space=pltpu.SMEM)
    anywhere = pl.BlockSpec(memory_space=pl.ANY)

    def call(kernel, outs, specs, terms, out_specs=vm, grid=(), scratch=()):
        return pl.pallas_call(
            kernel,
            out_shape=outs,
            in_specs=specs,
            out_specs=out_specs if not isinstance(outs, tuple) else (out_specs,) * len(outs),
            grid=grid,
            scratch_shapes=scratch,
            cost_estimate=pl.CostEstimate(
                flops=terms * 4 * rows * rows * width, bytes_accessed=2 << 20, transcendentals=0
            ),
            compiler_params=pltpu.CompilerParams(vmem_limit_bytes=32 << 20),
        )

    def bf(n):
        return jax.ShapeDtypeStruct((n, width), jnp.bfloat16)

    full = jax.ShapeDtypeStruct((rows, width), jnp.float32)

    cut = rows // 2
    pieces = (own_i[:half], own_i[half:], own_t[:cut])
    out = [move(p, t) for p, t in zip(pieces, MOVE_OUT)]
    straight = move(own_t[cut:], MOVE_STRAIGHT)
    far = []
    for q, o, p, t in zip(plane, out, pieces, MOVE_ON):
        relay = (x == q).astype(jnp.int32).reshape(1)
        far.append(move(call(relay_kernel, bf(p.shape[0]), [sm] + [vm] * 2, 0)(relay, o, p), t))
    near = move(call(after_kernel, bf(rows - cut), [vm, anywhere], 0)(own_t, out[2]), MOVE_NEAR)
    swap = call(swap_images, bf(rows), [sm] + [vm] * 5, 0)(where, out[0], far[0], out[1], far[1], own_i)
    i1 = move(swap, MOVE_SWAP)
    done = call(all_kernel, jax.ShapeDtypeStruct((8, 128), jnp.float32), [anywhere] * 3, 20)(far[2], straight, swap)
    t2, part = call(
        part_kernel, (bf(rows), full), [sm, anywhere] + [vm] * 9, 60, scratch=[pltpu.VMEM((rows, width), jnp.bfloat16)]
    )(where, done, out[0], far[0], out[1], far[1], out[2], far[2], straight, near, own_i)
    code = call(text_kernel, bf(rows + EXTRA), [vm] * 3, 1)(part, i1, t2)
    count = lax.axis_size("group")
    got = lax.ppermute(code, "group", [(s, (s + 1) % count) for s in range(count)])
    t1 = move(call(swap_texts, bf(rows), [sm, anywhere] + [vm] * 2, 0)(where, code, t2, own_t), MOVE_SWAP)
    image_grad = call(image_kernel, full, [vm] * 4, 0)(own_i, own_t, t1, t2)
    step = rows // 4
    text_grad = call(
        read_kernel, full, [vm], 0, out_specs=pl.BlockSpec((step, width), lambda n: (n, 0)), grid=(rows // step,)
    )(got)
    return image_grad.reshape(images.shape), text_grad.reshape(texts.shape)


def solution(mesh):
    spec = P("blk", "group", None, None)
    return jax.shard_map(body, mesh=mesh, in_specs=(spec, spec), out_specs=(spec, spec), check_vma=False)
```
